128 devices in a mesh: section: 2 (over y_lo), expert: 16 (over z, y_hi, core), dp: 4 (over x).
Axes of the slice: x: 4, y: 4 (y_hi: 2, y_lo: 2; y = y_hi * 2 + y_lo), z: 4, core: 2. Of those that a mesh axis runs over, the one named last changes fastest.
Arguments:
- residual: bfloat16 [16384, 2048], P(('section', 'expert', 'dp')), may hold values from -12 to 12
- queries: bfloat16 [16384, 1024], P(('section', 'expert', 'dp')), may hold values from -6 to 6
- attn_keys: bfloat16 [16384, 1024], P(('section', 'expert', 'dp')), may hold values from -6 to 6
- attn_values: bfloat16 [16384, 1024], P(('section', 'expert', 'dp')), may hold values from -6 to 6
- out_weight: bfloat16 [1024, 2048], P('expert'), may hold values from -0.1875 to 0.1875
- norm_gain: float32 [2048], replicated, may hold values from 0.25 to 1.75
- gate_weight: bfloat16 [16, 2048, 4096], P('expert', None, 'dp'), may hold values from -0.125 to 0.125
- up_weight: bfloat16 [16, 2048, 4096], P('expert', None, 'dp'), may hold values from -0.125 to 0.125
- down_weight: bfloat16 [16, 4096, 2048], P('expert', 'dp'), may hold values from -0.09375 to 0.09375
- expert_ids: int32 [16384, 1], P(('section', 'expert', 'dp')), may hold values from 0 to 15; in each aligned block of 128 rows (0 to 127, 128 to 255, ...) at most 16 rows name the same one
- out_grad: bfloat16 [16384, 2048], P(('section', 'expert', 'dp')), may hold values from -6 to 6
Outputs:
- layer_out: bfloat16 [16384, 2048], P(('section', 'expert', 'dp'))
- resid_grad: bfloat16 [16384, 2048], P(('section', 'expert', 'dp'))
- query_grad: bfloat16 [16384, 1024], P(('section', 'expert', 'dp'))
- key_grad: bfloat16 [16384, 1024], P(('section', 'expert', 'dp'))
- value_grad: bfloat16 [16384, 1024], P(('section', 'expert', 'dp'))
- weight_grad: float32 [1024, 2048], P('expert')
The draws below stay inside these ranges and needn't reach their ends.
Inputs may be any that keep to these rules, and one draw needn't show every extreme that they name: `expert_ids`: no expert is named by more than 16 of the 128 rows of one device (an aligned block); in every draw some block names one expert exactly 16 times.
All inputs are finite; a program needn't handle non-finite values.
Results may differ from the reference program's by a relative error of at most 0.023.
Values may be sent and summed in bfloat16 or wider, within the bound.
No kernel may reach another device: no remote copies, remote signals or barrier semaphores. Data moves between devices by JAX's collectives and lax.ppermute only.
A program may use at most 128 MiB of HBM per device.

```python
import math
import jax
import jax.numpy as jnp
import numpy as np
from jax import lax

D = 2048
HEADS = 8
HEAD = 128
A = 1024
FF = 4096
EXPERTS = 16
TOK_DEV = 128
CAP = 16
LEN = 512
SEQS = 32
TOKENS = 16384
N_DP = 4


def query_key_pair(key):
    base_query = jnp.clip(jax.random.normal(jax.random.fold_in(key, 71), (TOKENS, A), jnp.float32) * 1.3, -6.0, 6.0)
    base_key = jnp.clip(jax.random.normal(jax.random.fold_in(key, 72), (TOKENS, A), jnp.float32) * 1.3, -6.0, 6.0)
    return (base_query, base_key)


def draw_queries(key, part):
    return query_key_pair(key)[0].astype(jnp.bfloat16)


def draw_attn_keys(key, part):
    return query_key_pair(key)[1].astype(jnp.bfloat16)


def draw_residual(key, part):
    base_draw = jax.random.normal(jax.random.fold_in(key, 81), (TOKENS, D), jnp.float32)
    row_scale = jnp.exp(jax.random.uniform(jax.random.fold_in(key, 82), (TOKENS, 1), jnp.float32, -0.7, 0.7))
    column_scale = jnp.exp(jax.random.uniform(jax.random.fold_in(key, 83), (1, D), jnp.float32, -0.7, 0.7))
    return jnp.clip(base_draw * row_scale * column_scale, -12.0, 12.0).astype(jnp.bfloat16)


def shard_levels(stream_key, shape, cuts, least, top_value):
    gain = 1.0
    for dim, shards_of in cuts:
        heights = jax.random.uniform(jax.random.fold_in(jax.random.fold_in(stream_key, 6), dim), (shards_of,), jnp.float32, least / len(cuts), top_value / len(cuts))
        gain = gain * jnp.repeat(jnp.exp(heights), shape[dim] // shards_of).reshape((-1,) + (1,) * (len(shape) - 1 - dim))
    return gain


def routed_block(rng, own, number, rows, amount, top, most, slope):
    ranking = jax.random.permutation(rng, amount)
    crowded, ordinary = portions_of(amount, rows * top, most, slope, True), portions_of(amount, rows * top, most, slope, False)
    places = jnp.arange(amount)

    def named(tallies, rotation):
        used = int((tallies > 0).sum())
        fixed = max(1, used // 4)
        moved = fixed + (places - fixed + rotation * (used - fixed)) % max(1, amount - fixed)
        return jnp.zeros((amount,), jnp.int32).at[ranking[jnp.where(places < fixed, places, moved)]].set(jnp.asarray(tallies, jnp.int32))

    tallies = jnp.where(number % 4 == 0, named(crowded, number // 4), named(ordinary, number - number // 4 - 1))
    mixed = jax.random.permutation(jax.random.fold_in(own, 3), amount)
    source_of, sink = mixed[0:amount // 2 * 2:2], mixed[1:amount // 2 * 2:2]
    margin = jnp.minimum(tallies[source_of] - 1, most - tallies[sink]) // 2
    margin = jnp.where((source_of == ranking[0]) | (sink == ranking[0]) | (tallies[sink] == 0), 0, jnp.maximum(margin, 0))
    moved = jax.random.randint(jax.random.fold_in(own, 4), (amount // 2,), 0, 1 << 20) % (margin + 1)
    tallies = tallies.at[source_of].add(-moved).at[sink].add(moved)
    members = jnp.searchsorted(jnp.cumsum(tallies), jnp.arange(rows * top), side="right").astype(jnp.int32)
    table = members.reshape(top, rows).T
    table = table[jax.random.permutation(jax.random.fold_in(own, 1), rows)]
    rotation = jax.random.randint(jax.random.fold_in(own, 2), (rows, 1), 0, top)
    return jnp.take_along_axis(table, (jnp.arange(top)[None, :] + rotation) % top, axis=1)


def portions_of(count, total, limit, skew, full):
    weights = [(1 << 20) // math.isqrt(rank ** skew) + 1 for rank in range(1, count + 1)]
    largest = limit if full else min(limit, max(-(-total // count), total * weights[0] // sum(weights)))
    least = 1 if total - largest >= count - 1 else 0
    counts, surplus = [largest] + [least] * (count - 1), total - largest - least * (count - 1)
    while surplus > 0:
        movable = [i for i in range(1, count) if counts[i] < largest] or [i for i in range(1, count) if counts[i] < limit]
        whole, left = sum([weights[i] for i in movable]), surplus
        for i in movable:
            addition = min(limit - counts[i], max(1, left * weights[i] // whole), surplus)
            counts[i] = counts[i] + addition
            surplus = surplus - addition
    return np.array(counts)


def bell_draw(stream_key, dims, scale, most, shards=(), kind=jnp.bfloat16):
    factor_of = shard_levels(stream_key, dims, shards, -0.22, 0.18) if shards else 1.0
    values = jax.random.normal(stream_key, dims, jnp.float32) * scale * factor_of
    return jnp.minimum(jnp.maximum(values, -most), most).astype(kind)


def setup_inputs(seed: int = 0) -> dict:
    seeds = jax.random.split(jax.random.key(seed), 12)
    residual = draw_residual(jax.random.fold_in(seeds[11], 71), 0)
    queries = draw_queries(jax.random.fold_in(seeds[11], 71), 0)
    attn_keys = draw_attn_keys(jax.random.fold_in(seeds[11], 71), 0)
    attn_values = bell_draw(seeds[3], (TOKENS, A), 1.0, 6.0, ((0, 128),))
    out_weight = bell_draw(seeds[4], (A, D), A ** -0.5, 0.1875, ((0, 16),))
    norm_gain = jnp.clip(1.0 + 0.15 * jax.random.normal(seeds[5], (D,), jnp.float32), 0.25, 1.75)
    gate_weight = bell_draw(seeds[6], (EXPERTS, D, FF), D ** -0.5, 0.125, ((0, 16), (2, 4)))
    up_weight = bell_draw(seeds[7], (EXPERTS, D, FF), D ** -0.5, 0.125, ((0, 16), (2, 4)))
    down_weight = bell_draw(seeds[8], (EXPERTS, FF, D), FF ** -0.5, 0.09375, ((0, 16), (1, 4)))
    expert_ids_keys = jax.random.split(jax.random.fold_in(seeds[9], 1), TOKENS // TOK_DEV)
    expert_ids_turns = jax.random.permutation(jax.random.fold_in(seeds[9], 3), TOKENS // TOK_DEV)
    expert_ids = jax.vmap(lambda own, number: routed_block(jax.random.fold_in(seeds[9], 2), own, number, TOK_DEV, EXPERTS, 1, CAP, 2))(expert_ids_keys, expert_ids_turns).reshape((TOKENS, 1))
    out_grad = bell_draw(seeds[10], (TOKENS, D), 1.0, 6.0, ((0, 128),))
    return {"residual": residual, "queries": queries, "attn_keys": attn_keys, "attn_values": attn_values, "out_weight": out_weight, "norm_gain": norm_gain, "gate_weight": gate_weight, "up_weight": up_weight, "down_weight": down_weight, "expert_ids": expert_ids, "out_grad": out_grad}


epsilon = 1e-06

def low_copy(values):
    return lax.optimization_barrier(values.astype(jnp.bfloat16)).astype(jnp.float32)

def seq_probs(query_block, key_block):
    query_heads = query_block.reshape(LEN, HEADS, HEAD).astype(jnp.float32)
    key_heads = key_block.reshape(LEN, HEADS, HEAD).astype(jnp.float32)
    scores = jnp.einsum('qhd,khd->hqk', query_heads, key_heads) * (1.0 / math.sqrt(HEAD))
    row_peak = lax.optimization_barrier(jnp.max(scores, axis=-1, keepdims=True))
    exp_scores = jnp.exp(scores - row_peak)
    return exp_scores / lax.optimization_barrier(jnp.sum(exp_scores, axis=-1, keepdims=True))

def seq_forward(operands):
    query_block, key_block, value_block = operands
    attn_probs = seq_probs(query_block, key_block)
    value_heads = value_block.reshape(LEN, HEADS, HEAD).astype(jnp.float32)
    mixed_rows = jnp.einsum('hqk,khd->qhd', low_copy(attn_probs), value_heads)
    return mixed_rows.reshape(LEN, A).astype(jnp.bfloat16)

def seq_backward(operands):
    query_block, key_block, value_block, grad_block = operands
    attn_probs = seq_probs(query_block, key_block)
    probs_low = low_copy(attn_probs)
    inv_root = 1.0 / math.sqrt(HEAD)
    query_heads = query_block.reshape(LEN, HEADS, HEAD).astype(jnp.float32)
    key_heads = key_block.reshape(LEN, HEADS, HEAD).astype(jnp.float32)
    value_heads = value_block.reshape(LEN, HEADS, HEAD).astype(jnp.float32)
    grad_heads = grad_block.reshape(LEN, HEADS, HEAD).astype(jnp.float32)
    grad_probs = jnp.einsum('qhd,khd->hqk', grad_heads, value_heads)
    row_delta = lax.optimization_barrier(jnp.sum(attn_probs * grad_probs, axis=-1, keepdims=True))
    grad_scores = low_copy(attn_probs * (grad_probs - row_delta))
    query_grad = (jnp.einsum('hqk,khd->qhd', grad_scores, key_heads) * inv_root).reshape(LEN, A)
    key_grad = (jnp.einsum('hqk,qhd->khd', grad_scores, query_heads) * inv_root).reshape(LEN, A)
    value_grad = jnp.einsum('hqk,qhd->khd', probs_low, grad_heads).reshape(LEN, A)
    return (query_grad.astype(jnp.bfloat16), key_grad.astype(jnp.bfloat16), value_grad.astype(jnp.bfloat16))

def expert_forward(operands):
    row_block, gate_local, up_local, down_local = operands
    gate_pre = jnp.dot(row_block, gate_local, preferred_element_type=jnp.float32)
    up_pre = jnp.dot(row_block, up_local, preferred_element_type=jnp.float32)
    activated = (jax.nn.silu(gate_pre) * up_pre).astype(jnp.bfloat16)
    block_width = FF // N_DP
    running = jnp.zeros((row_block.shape[0], D), jnp.float32)
    for quarter in range(N_DP):
        lower_edge = quarter * block_width
        piece_sum = jnp.dot(activated[:, lower_edge:lower_edge + block_width], down_local[lower_edge:lower_edge + block_width], preferred_element_type=jnp.float32)
        running = running + low_copy(piece_sum)
    return running.astype(jnp.bfloat16)

def expert_backward(operands):
    row_block, grad_block, gate_local, up_local, down_local = operands
    gate_pre = jnp.dot(row_block, gate_local, preferred_element_type=jnp.float32)
    up_pre = jnp.dot(row_block, up_local, preferred_element_type=jnp.float32)
    sigmoid_gate = jax.nn.sigmoid(gate_pre)
    grad_act = lax.dot_general(grad_block, down_local, (((1,), (1,)), ((), ())), preferred_element_type=jnp.float32)
    grad_gate = (grad_act * up_pre * sigmoid_gate * (1.0 + gate_pre * (1.0 - sigmoid_gate))).astype(jnp.bfloat16)
    grad_up = (grad_act * jax.nn.silu(gate_pre)).astype(jnp.bfloat16)
    block_width = FF // N_DP
    running = jnp.zeros((row_block.shape[0], D), jnp.float32)
    for quarter in range(N_DP):
        lower_edge = quarter * block_width
        upper_edge = lower_edge + block_width
        piece_sum = lax.dot_general(grad_gate[:, lower_edge:upper_edge], gate_local[:, lower_edge:upper_edge], (((1,), (1,)), ((), ())), preferred_element_type=jnp.float32)
        piece_sum = piece_sum + lax.dot_general(grad_up[:, lower_edge:upper_edge], up_local[:, lower_edge:upper_edge], (((1,), (1,)), ((), ())), preferred_element_type=jnp.float32)
        running = running + low_copy(piece_sum)
    return running.astype(jnp.bfloat16)

def reference(residual, queries, attn_keys, attn_values, out_weight, norm_gain, gate_weight, up_weight, down_weight, expert_ids, out_grad):
    tiled = (SEQS, LEN, A)
    attended = lax.map(seq_forward, (queries.reshape(tiled), attn_keys.reshape(tiled), attn_values.reshape(tiled))).reshape(TOKENS, A)
    hidden = residual.astype(jnp.float32) + jnp.dot(attended, out_weight, preferred_element_type=jnp.float32)
    inv_rms = lax.rsqrt(lax.optimization_barrier(jnp.mean(hidden * hidden, axis=-1, keepdims=True)) + epsilon)
    unit_rows = hidden * inv_rms
    normed = (unit_rows * norm_gain).astype(jnp.bfloat16)
    expert_of = expert_ids[:, 0].astype(jnp.int32)
    onehot = (expert_of[:, None] == jnp.arange(EXPERTS, dtype=jnp.int32)[None, :]).astype(jnp.int32)
    per_device = onehot.reshape(-1, TOK_DEV, EXPERTS)
    before = jnp.cumsum(per_device, axis=1) - per_device
    rank_index = lax.optimization_barrier(jnp.sum(before * per_device, axis=-1)).reshape(-1)
    device_of = jnp.arange(TOKENS, dtype=jnp.int32) // TOK_DEV
    position = (device_of * CAP + rank_index).astype(jnp.int32)
    slots_all = TOKENS // TOK_DEV * CAP
    empty_buckets = jnp.zeros((EXPERTS, slots_all, D), jnp.bfloat16)
    buckets = empty_buckets.at[expert_of, position].set(normed)
    expert_rows = lax.map(expert_forward, (buckets, gate_weight, up_weight, down_weight))
    expert_back = expert_rows[expert_of, position]
    layer_out = (hidden + expert_back.astype(jnp.float32)).astype(jnp.bfloat16)
    grad_buckets = empty_buckets.at[expert_of, position].set(out_grad)
    grad_rows = lax.map(expert_backward, (buckets, grad_buckets, gate_weight, up_weight, down_weight))
    grad_normed = grad_rows[expert_of, position].astype(jnp.float32)
    scaled = grad_normed * norm_gain
    resid_grad = (out_grad.astype(jnp.float32) + inv_rms * (scaled - unit_rows * lax.optimization_barrier(jnp.mean(scaled * unit_rows, axis=-1, keepdims=True)))).astype(jnp.bfloat16)
    weight_grad = lax.dot_general(attended, resid_grad, (((0,), (0,)), ((), ())), preferred_element_type=jnp.float32)
    grad_attended = lax.dot_general(resid_grad, out_weight, (((1,), (1,)), ((), ())), preferred_element_type=jnp.float32).astype(jnp.bfloat16)
    query_grad, key_grad, value_grad = lax.map(seq_backward, (queries.reshape(tiled), attn_keys.reshape(tiled), attn_values.reshape(tiled), grad_attended.reshape(tiled)))
    return (layer_out, resid_grad, query_grad.reshape(TOKENS, A), key_grad.reshape(TOKENS, A), value_grad.reshape(TOKENS, A), weight_grad)
```

```python
import math

import jax
import jax.numpy as jnp
from jax import lax
from jax.experimental import pallas as pl
from jax.experimental.pallas import tpu as pltpu
from jax.sharding import PartitionSpec as P

D = 2048
HEADS = 8
HEAD = 128
A = 1024
EXPERTS = 16
CAP = 16
CHUNKS = 2
SLOTS = CAP // CHUNKS
ROWS = 128
HALF = ROWS // 2
EPSILON = 1e-06
INV_ROOT = 1.0 / math.sqrt(HEAD)
F32 = jnp.float32
BF16 = jnp.bfloat16


def dot_nn(a, b):
    return lax.dot_general(a, b, (((1,), (0,)), ((), ())), preferred_element_type=F32)


def dot_nt(a, b):
    return lax.dot_general(a, b, (((1,), (1,)), ((), ())), preferred_element_type=F32)


def dot_tn(a, b):
    return lax.dot_general(a, b, (((0,), (0,)), ((), ())), preferred_element_type=F32)


def to_right(block):
    return lax.ppermute(block, "dp", [(i, (i + 1) % 4) for i in range(4)])


def to_left(block):
    return lax.ppermute(block, "dp", [(i, (i + 3) % 4) for i in range(4)])


def along_z(block, back):
    perm = [(e, ((e // 4 - back) % 4) * 4 + e % 4) for e in range(EXPERTS)]
    return lax.ppermute(block, "expert", perm)


def across_y(block):
    return lax.ppermute(block, "expert", [(e, e ^ 2) for e in range(EXPERTS)])


def across_core(block):
    return lax.ppermute(block, "expert", [(e, e ^ 1) for e in range(EXPERTS)])


def ring_gather(block, half):
    left = to_right(block)
    right = to_left(block)
    opp_a = to_right(left[:half])
    opp_b = to_left(right[half:])
    return left, right, opp_a, opp_b


def ring_sum(own, keep_right, keep_left, send_right, send_left):
    half = keep_right.shape[-2]
    from_left = to_right(send_right)
    from_right = to_left(send_left)
    first = lax.slice_in_dim(from_left, 0, half, axis=-2)
    second = lax.slice_in_dim(from_right, 0, half, axis=-2)
    low_left = to_right((keep_right.astype(F32) + first.astype(F32)).astype(BF16))
    high_right = to_left((keep_left.astype(F32) + second.astype(F32)).astype(BF16))
    high_left = lax.slice_in_dim(from_left, half, 2 * half, axis=-2)
    low_right = lax.slice_in_dim(from_right, half, 2 * half, axis=-2)
    others = jnp.concatenate(
        [low_left.astype(F32) + low_right.astype(F32), high_left.astype(F32) + high_right.astype(F32)],
        axis=-2,
    )
    return own.astype(F32) + others


def swap_experts(rows):
    out = lax.all_to_all(
        rows.reshape(EXPERTS, SLOTS, D), "expert", split_axis=0, concat_axis=0, tiled=True
    )
    return out.reshape(ROWS, D)


def probs_of(q, keys):
    scores = dot_nt(q, keys) * INV_ROOT
    peak = jnp.max(scores, axis=-1, keepdims=True)
    e = jnp.exp(scores - peak)
    return e / jnp.sum(e, axis=-1, keepdims=True)


def attend_kernel(q, k0, k1, k2, k3, k4, v0, v1, v2, v3, v4, out):
    keys = jnp.concatenate([r[...] for r in (k0, k1, k2, k3, k4)], axis=0)
    values = jnp.concatenate([r[...] for r in (v0, v1, v2, v3, v4)], axis=0)
    probs = probs_of(q[...], keys)
    out[...] = dot_nn(probs.astype(BF16), values).astype(BF16)


def attend_back_kernel(
    q, g, k0, k1, k2, k3, k4, v0, v1, v2, v3, v4, dq, own, keep_r, keep_l, send_r, send_l
):
    keys = jnp.concatenate([r[...] for r in (k0, k1, k2, k3, k4)], axis=0)
    values = jnp.concatenate([r[...] for r in (v0, v1, v2, v3, v4)], axis=0)
    query = q[...]
    grad = g[...]
    probs = probs_of(query, keys)
    grad_probs = dot_nt(grad, values)
    delta = jnp.sum(probs * grad_probs, axis=-1, keepdims=True)
    grad_scores = (probs * (grad_probs - delta)).astype(BF16)
    dq[...] = (dot_nn(grad_scores, keys) * INV_ROOT).astype(BF16)
    dk = (dot_tn(grad_scores, query) * INV_ROOT).astype(BF16)
    dv = dot_tn(probs.astype(BF16), grad).astype(BF16)
    for part, rows in ((0, dk), (1, dv)):
        own[part] = rows[0:128]
        keep_r[part] = rows[256:320]
        keep_l[part] = rows[192:256]
        send_r[part, 0:64] = rows[384:448]
        send_r[part, 64:128] = rows[320:384]
        send_l[part, 0:64] = rows[448:512]
        send_l[part, 64:128] = rows[128:192]


def head_specs():
    query = pl.BlockSpec((ROWS, HEAD), lambda h: (0, h))
    sizes = (ROWS, ROWS, ROWS, HALF, HALF)
    keys = [pl.BlockSpec((n, HEAD), lambda h: (0, h)) for n in sizes]
    values = [pl.BlockSpec((n, HEAD), lambda h: (0, h + HEADS)) for n in sizes]
    return query, keys, values


def attend(queries, kv):
    query, keys, values = head_specs()
    return pl.pallas_call(
        attend_kernel,
        grid=(HEADS,),
        in_specs=[query, *keys, *values],
        out_specs=query,
        out_shape=jax.ShapeDtypeStruct((ROWS, A), BF16),
        cost_estimate=pl.CostEstimate(
            flops=4 * HEADS * ROWS * 512 * HEAD, bytes_accessed=3 << 20, transcendentals=HEADS * ROWS * 512
        ),
    )(queries, *kv, *kv)


def attend_back(queries, grads, kv):
    query, keys, values = head_specs()

    def piece(n):
        return pl.BlockSpec((2, n, HEAD), lambda h: (0, 0, h)), jax.ShapeDtypeStruct((2, n, A), BF16)

    pieces = [piece(n) for n in (ROWS, HALF, HALF, ROWS, ROWS)]
    return pl.pallas_call(
        attend_back_kernel,
        grid=(HEADS,),
        in_specs=[query, query, *keys, *values],
        out_specs=[query, *(s for s, _ in pieces)],
        out_shape=[jax.ShapeDtypeStruct((ROWS, A), BF16), *(s for _, s in pieces)],
        cost_estimate=pl.CostEstimate(
            flops=12 * HEADS * ROWS * 512 * HEAD, bytes_accessed=6 << 20, transcendentals=HEADS * ROWS * 512
        ),
    )(queries, grads, *kv, *kv)


def gathered_rows(block):
    left, right, opp_a, opp_b = ring_gather(block, HALF)
    return jnp.concatenate(
        [block, right[:HALF], left[HALF:], opp_a, right[HALF:], opp_b, left[:HALF]], axis=0
    )


def summed_rows(part):
    part = part.astype(BF16)
    return ring_sum(part[0:128], part[128:192], part[192:256], part[256:384], part[384:512]).astype(BF16)


def shards(
    residual,
    queries,
    attn_keys,
    attn_values,
    out_weight,
    norm_gain,
    gate_weight,
    up_weight,
    down_weight,
    expert_ids,
    out_grad,
):
    gate, up, down = gate_weight[0], up_weight[0], down_weight[0]

    kv_own = jnp.concatenate([attn_keys, attn_values], axis=1)
    kv = (kv_own, *ring_gather(kv_own, HALF))

    expert_of = expert_ids[:, 0]
    onehot = (expert_of[:, None] == jnp.arange(EXPERTS, dtype=jnp.int32)[None, :]).astype(BF16)
    row = jnp.arange(ROWS, dtype=jnp.int32)
    earlier_mask = (row[:, None] > row[None, :]).astype(BF16)
    earlier = dot_nn(earlier_mask, onehot)
    rank = jnp.sum(earlier * onehot.astype(F32), axis=1).astype(jnp.int32)
    slot = (rank // SLOTS) * ROWS + expert_of * SLOTS + rank % SLOTS
    place = (jnp.arange(CHUNKS * ROWS, dtype=jnp.int32)[:, None] == slot[None, :]).astype(BF16)

    grad_rows = []
    for c in range(CHUNKS):
        buffer = dot_nn(place[c * ROWS : (c + 1) * ROWS], out_grad).astype(BF16)
        grad_rows.append(gathered_rows(swap_experts(buffer)))

    y_pair = jnp.concatenate([out_weight, across_y(out_weight)], axis=0)
    z_all = jnp.concatenate([y_pair, *(along_z(y_pair, 4 - k) for k in (1, 2, 3))], axis=0)
    full_out = jnp.concatenate([z_all, across_core(z_all)], axis=0)
    me = lax.axis_index("expert")
    block = jnp.arange(EXPERTS, dtype=jnp.int32)
    source = ((me // 4 - (block // 2) % 4) % 4) * 4 + ((me % 4) // 2 ^ (block % 2)) * 2 + (me % 2 ^ (block // 8))
    column = jnp.arange(A, dtype=jnp.int32)
    wanted = (source[:, None] * 64 + jnp.arange(64, dtype=jnp.int32)[None, :]).reshape(A)
    reorder = (column[:, None] == wanted[None, :]).astype(BF16)

    attended = attend(queries, kv)
    attended_rel = dot_nn(attended, reorder).astype(BF16)
    hidden = residual.astype(F32) + dot_nn(attended_rel, full_out)
    inv_rms = lax.rsqrt(jnp.mean(hidden * hidden, axis=-1, keepdims=True) + EPSILON)
    unit_rows = hidden * inv_rms
    normed = (unit_rows * norm_gain).astype(BF16)

    grad_back = []
    out_back = []
    activated_all = []
    for c in range(CHUNKS):
        buffer = dot_nn(place[c * ROWS : (c + 1) * ROWS], normed).astype(BF16)
        rows = gathered_rows(swap_experts(buffer))
        grad_act = dot_nt(grad_rows[c], down)
        gate_pre = dot_nn(rows, gate)
        up_pre = dot_nn(rows, up)
        sigmoid_gate = jax.nn.sigmoid(gate_pre)
        silu_gate = gate_pre * sigmoid_gate
        activated_all.append((silu_gate * up_pre).astype(BF16))
        grad_gate = (
            grad_act * up_pre * sigmoid_gate * (1.0 + gate_pre * (1.0 - sigmoid_gate))
        ).astype(BF16)
        grad_up = (grad_act * silu_gate).astype(BF16)
        part = dot_nt(grad_gate, gate) + dot_nt(grad_up, up)
        grad_back.append(swap_experts(summed_rows(part)))
    for c in range(CHUNKS):
        out_back.append(swap_experts(summed_rows(dot_nn(activated_all[c], down))))

    grad_normed = dot_tn(place, jnp.concatenate(grad_back, axis=0))
    scaled = grad_normed * norm_gain
    resid_grad = (
        out_grad.astype(F32)
        + inv_rms * (scaled - unit_rows * jnp.mean(scaled * unit_rows, axis=-1, keepdims=True))
    ).astype(BF16)

    grad_rel = dot_nt(resid_grad, full_out).astype(BF16)
    grad_attended = dot_nt(grad_rel, reorder).astype(BF16)
    query_grad, own, keep_r, keep_l, send_r, send_l = attend_back(queries, grad_attended, kv)
    kv_grad = ring_sum(own, keep_r, keep_l, send_r, send_l).astype(BF16)

    partial = dot_tn(attended_rel, resid_grad).astype(BF16).reshape(2, 4, 128, D)
    partial = partial[0].astype(F32) + across_core(partial[1]).astype(F32)
    low = partial.astype(BF16)
    partial = partial[0] + sum(along_z(low[k], k).astype(F32) for k in (1, 2, 3))
    partial = partial[:64] + across_y(partial[64:].astype(BF16)).astype(F32)
    pieces = lax.all_to_all(
        partial.astype(BF16).reshape(8, 8, D), ("section", "dp"), split_axis=0, concat_axis=0, tiled=True
    )
    piece = pieces.astype(F32).sum(axis=0).astype(BF16)
    weight_grad = lax.all_to_all(
        jnp.broadcast_to(piece[None], (8, 8, D)), ("section", "dp"), split_axis=0, concat_axis=0, tiled=True
    )
    weight_grad = weight_grad.reshape(64, D).astype(F32)

    expert_back = dot_tn(place, jnp.concatenate(out_back, axis=0))
    layer_out = (hidden + expert_back).astype(BF16)
    return (layer_out, resid_grad, query_grad, kv_grad[0], kv_grad[1], weight_grad)


def solution(mesh):
    rows = P(("section", "expert", "dp"), None)
    return jax.shard_map(
        shards,
        mesh=mesh,
        in_specs=(
            rows,
            rows,
            rows,
            rows,
            P("expert", None),
            P(),
            P("expert", None, "dp"),
            P("expert", None, "dp"),
            P("expert", "dp", None),
            rows,
            rows,
        ),
        out_specs=(rows, rows, rows, rows, rows, P("expert", None)),
        check_vma=False,
    )
```

```python
import functools
import math

import jax
import jax.numpy as jnp
from jax import lax
from jax.experimental import pallas as pl
from jax.experimental.pallas import tpu as pltpu
from jax.sharding import PartitionSpec as P

D = 2048
HEADS = 8
HEAD = 128
A = 1024
EXPERTS = 16
CAP = 16
ROWS = 128
POOL = EXPERTS * CAP
HALF = POOL // 2
QUARTER = D // 4
EPSILON = 1e-06
INV_ROOT = 1.0 / math.sqrt(HEAD)
F32 = jnp.float32
BF16 = jnp.bfloat16


def dot_nn(a, b):
    return lax.dot_general(a, b, (((1,), (0,)), ((), ())), preferred_element_type=F32)


def dot_nt(a, b):
    return lax.dot_general(a, b, (((1,), (1,)), ((), ())), preferred_element_type=F32)


def dot_tn(a, b):
    return lax.dot_general(a, b, (((0,), (0,)), ((), ())), preferred_element_type=F32)


def along_x(block, step):
    return lax.ppermute(block, "dp", [(i, (i + step) % 4) for i in range(4)])


def along_z(block, step):
    perm = [(e, ((e // 4 + step) % 4) * 4 + e % 4) for e in range(EXPERTS)]
    return lax.ppermute(block, "expert", perm)


def after(value, *tokens):
    for token in tokens:
        entry = token[(0,) * token.ndim]
        value = jnp.where(entry == entry, value, jnp.zeros_like(value))
    return value


def across_y(block):
    return lax.ppermute(block, "expert", [(e, e ^ 2) for e in range(EXPERTS)])


def across_core(block):
    return lax.ppermute(block, "expert", [(e, e ^ 1) for e in range(EXPERTS)])


def swap_experts(rows):
    out = lax.all_to_all(
        rows.reshape(EXPERTS, CAP, D), "expert", split_axis=0, concat_axis=0, tiled=True
    )
    return out.reshape(POOL, D)


def probs_of(q, keys):
    scores = dot_nt(q, keys) * INV_ROOT
    peak = jnp.max(scores, axis=-1, keepdims=True)
    e = jnp.exp(scores - peak)
    return e / jnp.sum(e, axis=-1, keepdims=True)


def attend_kernel(q, kv, out):
    for h in range(HEADS):
        cols = slice(h * HEAD, (h + 1) * HEAD)
        value_cols = slice(A + h * HEAD, A + (h + 1) * HEAD)
        probs = probs_of(q[:, cols], kv[:, cols])
        out[:, cols] = dot_nn(probs.astype(BF16), kv[:, value_cols]).astype(BF16)


def attend_back_kernel(lane, q, g, kv, dq, own, right, opp, left, terms):
    for h in range(HEADS):
        cols = slice(h * HEAD, (h + 1) * HEAD)
        value_cols = slice(A + h * HEAD, A + (h + 1) * HEAD)
        keys = kv[:, cols]
        query = q[:, cols]
        grad = g[:, cols]
        probs = probs_of(query, keys)
        grad_probs = dot_nt(grad, kv[:, value_cols])
        delta = jnp.sum(probs * grad_probs, axis=-1, keepdims=True)
        grad_scores = (probs * (grad_probs - delta)).astype(BF16)
        dq[:, cols] = (dot_nn(grad_scores, keys) * INV_ROOT).astype(BF16)
        dk = (dot_tn(grad_scores, query) * INV_ROOT).astype(BF16)
        dv = dot_tn(probs.astype(BF16), grad).astype(BF16)
        for i in range(4):
            terms[i, :, cols] = dk[i * ROWS : (i + 1) * ROWS]
            terms[i, :, value_cols] = dv[i * ROWS : (i + 1) * ROWS]
    for step, out in enumerate((own, right, opp, left)):
        out[...] = terms[(lane[0] + step) % 4]


WHOLE = pl.BlockSpec(memory_space=pltpu.VMEM)
PARAMS = pltpu.CompilerParams(vmem_limit_bytes=32 << 20)


def attend(queries, kv):
    return pl.pallas_call(
        attend_kernel,
        in_specs=[WHOLE] * 2,
        out_specs=WHOLE,
        out_shape=jax.ShapeDtypeStruct((ROWS, A), BF16),
        compiler_params=PARAMS,
        cost_estimate=pl.CostEstimate(
            flops=4 * HEADS * ROWS * 512 * HEAD, bytes_accessed=3 << 20, transcendentals=HEADS * ROWS * 512
        ),
    )(queries, kv)


def attend_back(lane, queries, grads, kv):
    return pl.pallas_call(
        attend_back_kernel,
        in_specs=[pl.BlockSpec(memory_space=pltpu.SMEM)] + [WHOLE] * 3,
        out_specs=[WHOLE] * 5,
        out_shape=[jax.ShapeDtypeStruct((ROWS, A), BF16)]
        + [jax.ShapeDtypeStruct((ROWS, 2 * A), BF16)] * 4,
        scratch_shapes=[pltpu.VMEM((4, ROWS, 2 * A), BF16)],
        compiler_params=PARAMS,
        cost_estimate=pl.CostEstimate(
            flops=12 * HEADS * ROWS * 512 * HEAD, bytes_accessed=6 << 20, transcendentals=HEADS * ROWS * 512
        ),
    )(lane.reshape(1), queries, grads, kv)


def expert(rows, grad_act, gate, up):
    gate_pre = dot_nn(rows, gate)
    up_pre = dot_nn(rows, up)
    sigmoid_gate = jax.nn.sigmoid(gate_pre)
    silu_gate = gate_pre * sigmoid_gate
    activated = (silu_gate * up_pre).astype(BF16)
    grad_gate = (grad_act * up_pre * sigmoid_gate * (1.0 + gate_pre * (1.0 - sigmoid_gate))).astype(BF16)
    grad_up = (grad_act * silu_gate).astype(BF16)
    return activated, (dot_nt(grad_gate, gate) + dot_nt(grad_up, up)).astype(BF16)


def project_others_kernel(lane, right, opp, left, down, out):
    step = pl.program_id(0)

    @pl.when(step == 0)
    def _():
        out[...] = dot_nn(right[...], down[...]).astype(BF16)

    @pl.when(step == 1)
    def _():
        out[...] = dot_nn(opp[...], down[...]).astype(BF16)

    @pl.when(step == 2)
    def _():
        out[...] = dot_nn(left[...], down[...]).astype(BF16)


def project_others(lane, right, opp, left, down):
    return pl.pallas_call(
        project_others_kernel,
        grid_spec=pltpu.PrefetchScalarGridSpec(
            num_scalar_prefetch=1,
            grid=(3,),
            in_specs=[WHOLE] * 4,
            out_specs=pl.BlockSpec((POOL, D), lambda i, lane: ((lane[0] + 1 + i) % 4, 0)),
        ),
        out_shape=jax.ShapeDtypeStruct((4 * POOL, D), BF16),
        compiler_params=pltpu.CompilerParams(vmem_limit_bytes=48 << 20),
        cost_estimate=pl.CostEstimate(flops=6 * POOL * D * A, bytes_accessed=8 << 20, transcendentals=0),
    )(lane.reshape(1), right, opp, left, down)


def project_own_kernel(lane, own, down, others, token, out):
    out[...] = dot_nn(own[...], down[...]).astype(BF16)


def project_own(lane, own, down, others, token):
    anywhere = pl.BlockSpec(memory_space=pl.ANY)
    return pl.pallas_call(
        project_own_kernel,
        grid_spec=pltpu.PrefetchScalarGridSpec(
            num_scalar_prefetch=1,
            grid=(1,),
            in_specs=[WHOLE, WHOLE, anywhere, anywhere],
            out_specs=pl.BlockSpec((POOL, D), lambda i, lane: (lane[0], 0)),
        ),
        out_shape=jax.ShapeDtypeStruct((4 * POOL, D), BF16),
        input_output_aliases={3: 0},
        compiler_params=pltpu.CompilerParams(vmem_limit_bytes=48 << 20),
        cost_estimate=pl.CostEstimate(flops=2 * POOL * D * A, bytes_accessed=5 << 20, transcendentals=0),
    )(lane.reshape(1), own, down, others, token)


def row_of(me, turn, flip, core):
    return (((me // 4 - turn) % 4) * 4 + ((me // 2 % 2) ^ flip) * 2 + (me % 2 ^ core)) * 64


def shards(
    residual,
    queries,
    attn_keys,
    attn_values,
    out_weight,
    norm_gain,
    gate_weight,
    up_weight,
    down_weight,
    expert_ids,
    out_grad,
):
    gate, up, down = gate_weight[0], up_weight[0], down_weight[0]
    lane = lax.axis_index("dp")

    kv = lax.all_gather(jnp.concatenate([attn_keys, attn_values], axis=1), "dp", axis=0, tiled=True)

    expert_of = expert_ids[:, 0]
    onehot = (expert_of[:, None] == jnp.arange(EXPERTS, dtype=jnp.int32)[None, :]).astype(BF16)
    row = jnp.arange(ROWS, dtype=jnp.int32)
    earlier_mask = (row[:, None] > row[None, :]).astype(BF16)
    earlier = dot_nn(earlier_mask, onehot)
    rank = jnp.sum(earlier * onehot.astype(F32), axis=1).astype(jnp.int32)
    slot = expert_of * CAP + rank
    place = (jnp.arange(POOL, dtype=jnp.int32)[:, None] == slot[None, :]).astype(BF16)

    low_z = jnp.concatenate([out_weight[:32], *(along_z(out_weight[:32], k) for k in (1, 2, 3))], axis=0)
    high_y = jnp.concatenate([out_weight[32:], across_y(out_weight[32:])], axis=0)
    near_out = jnp.concatenate(
        [low_z, across_y(low_z), high_y, *(along_z(high_y, k) for k in (1, 2, 3))], axis=0
    )
    far_out = across_core(near_out)
    me = lax.axis_index("expert")
    row = jnp.arange(A, dtype=jnp.int32)
    part = row % 256
    in_high = (row // 256) % 2
    turn = jnp.where(in_high == 1, part // 64, (part // 32) % 4)
    flip = jnp.where(in_high == 1, (part // 32) % 2, part // 128)
    wanted = row_of(me, turn, flip, row // 512) + in_high * 32 + row % 32
    reorder = (row[:, None] == wanted[None, :]).astype(BF16)

    grad_buffer = dot_nn(place, out_grad).astype(BF16)
    grad_rows = lax.all_gather(swap_experts(grad_buffer), "dp", axis=0, tiled=True)

    attended = attend(queries, kv)
    ordered = dot_nn(attended, reorder).astype(BF16)
    hidden = residual.astype(F32) + dot_nn(ordered[:, : A // 2], near_out) + dot_nn(ordered[:, A // 2 :], far_out)
    inv_rms = lax.rsqrt(jnp.mean(hidden * hidden, axis=-1, keepdims=True) + EPSILON)
    unit_rows = hidden * inv_rms
    normed = (unit_rows * norm_gain).astype(BF16)

    rows_own = swap_experts(dot_nn(place, normed).astype(BF16))
    rows_left, rows_right = along_x(rows_own, 1), along_x(rows_own, 3)
    grad_act = dot_nt(grad_rows, down).reshape(4, POOL, A)

    def act_of(step):
        return lax.dynamic_index_in_dim(grad_act, (lane + step) % 4, 0, keepdims=False)

    act_own, part_own = expert(rows_own, act_of(0), gate, up)
    opp_low = along_x(after(rows_left[:HALF], act_own), 1)
    opp_high = along_x(after(rows_right[HALF:], act_own), 3)
    act_left, part_left = expert(rows_left, act_of(3), gate, up)
    act_right, part_right = expert(rows_right, act_of(1), gate, up)
    rows_opp = after(jnp.concatenate([opp_low, opp_high], axis=0), part_left, part_right)
    act_opp, part_opp = expert(rows_opp, act_of(2), gate, up)

    from_left = along_x(jnp.concatenate([part_opp[:HALF], part_right[HALF:]], axis=0), 1)
    from_right = along_x(jnp.concatenate([part_opp[HALF:], part_left[:HALF]], axis=0), 3)
    out_others = project_others(lane, act_right, act_opp, act_left, down)
    keep_right = (part_right[:HALF].astype(F32) + from_left[:HALF].astype(F32)).astype(BF16)
    keep_left = (part_left[HALF:].astype(F32) + from_right[:HALF].astype(F32)).astype(BF16)
    low_left = along_x(after(keep_right, out_others), 1)
    high_right = along_x(after(keep_left, out_others), 3)
    low_sum = low_left.astype(F32) + from_right[HALF:].astype(F32)
    high_sum = high_right.astype(F32) + from_left[HALF:].astype(F32)
    own_sum = (part_own.astype(F32) + jnp.concatenate([low_sum, high_sum], axis=0)).astype(BF16)
    grad_back = swap_experts(own_sum)

    out_part = project_own(lane, act_own, down, out_others, own_sum)
    out_sum = lax.psum_scatter(out_part, "dp", scatter_dimension=0, tiled=True)
    out_back = swap_experts(out_sum)

    scaled = dot_tn(place, grad_back) * norm_gain
    resid_grad = (
        out_grad.astype(F32)
        + inv_rms * (scaled - unit_rows * jnp.mean(scaled * unit_rows, axis=-1, keepdims=True))
    ).astype(BF16)

    grad_attended = jnp.concatenate([dot_nt(resid_grad, near_out), dot_nt(resid_grad, far_out)], axis=1)
    grad_attended = dot_nt(grad_attended.astype(BF16), reorder).astype(BF16)
    query_grad, kv_own, kv_right, kv_opp, kv_left = attend_back(lane, queries, grad_attended, kv)
    kv_grad = (
        kv_own.astype(F32)
        + along_x(kv_opp, 2).astype(F32)
        + along_x(kv_right, 1).astype(F32)
        + along_x(kv_left, 3).astype(F32)
    ).astype(BF16)

    tile_attended = lax.all_gather(after(attended, part_left), "dp", axis=0, tiled=True)
    columns = lax.all_to_all(
        jnp.moveaxis(resid_grad.reshape(ROWS, 4, QUARTER), 1, 0), "dp", split_axis=0, concat_axis=0, tiled=True
    ).reshape(4 * ROWS, QUARTER)
    wanted = row_of(me, (row // 128) % 4, (row // 64) % 2, row // 512) + row % 64
    to_owner = (row[:, None] == wanted[None, :]).astype(BF16)
    tile_attended = dot_nn(after(tile_attended, query_grad), to_owner).astype(BF16)
    partial = dot_tn(tile_attended[:, A // 2 :], columns).astype(BF16)
    kept = dot_tn(tile_attended[:, : A // 2], columns)
    partial = (kept + across_core(partial).astype(F32)).reshape(4, 128, QUARTER)
    low = partial.astype(BF16)
    partial = partial[0] + sum(along_z(low[k], 4 - k).astype(F32) for k in (1, 2, 3))
    low = after(partial.astype(BF16), kv_grad)
    pair = [(i, i ^ 16) for i in range(2 * EXPERTS)]
    cross = [(i, i ^ 18) for i in range(2 * EXPERTS)]
    low = (
        partial[:64]
        + across_y(low[64:]).astype(F32)
        + lax.ppermute(low[:64], ("section", "expert"), pair).astype(F32)
        + lax.ppermute(low[64:], ("section", "expert"), cross).astype(F32)
    ).astype(BF16)
    low = after(low, out_back)
    weight_grad = jnp.zeros((64, D), F32)
    for step in range(4):
        piece = low if step == 0 else along_x(low, step)
        weight_grad = lax.dynamic_update_slice(
            weight_grad, piece.astype(F32), (0, ((lane - step) % 4) * QUARTER)
        )

    layer_out = (hidden + dot_tn(place, out_back)).astype(BF16)
    return (layer_out, resid_grad, query_grad, kv_grad[:, :A], kv_grad[:, A:], weight_grad)


def solution(mesh):
    rows = P(("section", "expert", "dp"), None)
    return jax.shard_map(
        shards,
        mesh=mesh,
        in_specs=(
            rows,
            rows,
            rows,
            rows,
            P("expert", None),
            P(),
            P("expert", None, "dp"),
            P("expert", None, "dp"),
            P("expert", "dp", None),
            rows,
            rows,
        ),
        out_specs=(rows, rows, rows, rows, rows, P("expert", None)),
        check_vma=False,
    )
```

```python
import functools
import math

import jax
import jax.numpy as jnp
from jax import lax
from jax.experimental import pallas as pl
from jax.experimental.pallas import tpu as pltpu
from jax.sharding import PartitionSpec as P

D = 2048
HEADS = 8
HEAD = 128
A = 1024
EXPERTS = 16
CAP = 16
ROWS = 128
POOL = EXPERTS * CAP
HALF = POOL // 2
QUARTER = D // 4
EPSILON = 1e-06
INV_ROOT = 1.0 / math.sqrt(HEAD)
F32 = jnp.float32
BF16 = jnp.bfloat16


def dot_nn(a, b):
    return lax.dot_general(a, b, (((1,), (0,)), ((), ())), preferred_element_type=F32)


def dot_nt(a, b):
    return lax.dot_general(a, b, (((1,), (1,)), ((), ())), preferred_element_type=F32)


def dot_tn(a, b):
    return lax.dot_general(a, b, (((0,), (0,)), ((), ())), preferred_element_type=F32)


def along_x(block, step):
    return lax.ppermute(block, "dp", [(i, (i + step) % 4) for i in range(4)])


def along_z(block, step):
    perm = [(e, ((e // 4 + step) % 4) * 4 + e % 4) for e in range(EXPERTS)]
    return lax.ppermute(block, "expert", perm)


def after(value, *tokens):
    for token in tokens:
        entry = token[(0,) * token.ndim]
        value = jnp.where(entry == entry, value, jnp.zeros_like(value))
    return value


def across_y(block):
    return lax.ppermute(block, "expert", [(e, e ^ 2) for e in range(EXPERTS)])


def across_core(block):
    return lax.ppermute(block, "expert", [(e, e ^ 1) for e in range(EXPERTS)])


def swap_experts(rows):
    out = lax.all_to_all(
        rows.reshape(EXPERTS, CAP, D), "expert", split_axis=0, concat_axis=0, tiled=True
    )
    return out.reshape(POOL, D)


def probs_of(q, keys):
    scores = dot_nt(q, keys) * INV_ROOT
    peak = jnp.max(scores, axis=-1, keepdims=True)
    e = jnp.exp(scores - peak)
    return e / jnp.sum(e, axis=-1, keepdims=True)


def attend_kernel(q, kv, out):
    for h in range(HEADS):
        cols = slice(h * HEAD, (h + 1) * HEAD)
        value_cols = slice(A + h * HEAD, A + (h + 1) * HEAD)
        probs = probs_of(q[:, cols], kv[:, cols])
        out[:, cols] = dot_nn(probs.astype(BF16), kv[:, value_cols]).astype(BF16)


def attend_back_kernel(lane, q, g, kv, token, dq, own, right, opp, left, terms):
    for h in range(HEADS):
        cols = slice(h * HEAD, (h + 1) * HEAD)
        value_cols = slice(A + h * HEAD, A + (h + 1) * HEAD)
        keys = kv[:, cols]
        query = q[:, cols]
        grad = g[:, cols]
        probs = probs_of(query, keys)
        grad_probs = dot_nt(grad, kv[:, value_cols])
        delta = jnp.sum(probs * grad_probs, axis=-1, keepdims=True)
        grad_scores = (probs * (grad_probs - delta)).astype(BF16)
        dq[:, cols] = (dot_nn(grad_scores, keys) * INV_ROOT).astype(BF16)
        dk = (dot_tn(grad_scores, query) * INV_ROOT).astype(BF16)
        dv = dot_tn(probs.astype(BF16), grad).astype(BF16)
        for i in range(4):
            terms[i, :, cols] = dk[i * ROWS : (i + 1) * ROWS]
            terms[i, :, value_cols] = dv[i * ROWS : (i + 1) * ROWS]
    for step, out in enumerate((own, right, opp, left)):
        out[...] = terms[(lane[0] + step) % 4]


WHOLE = pl.BlockSpec(memory_space=pltpu.VMEM)
PARAMS = pltpu.CompilerParams(vmem_limit_bytes=32 << 20)


def attend(queries, kv):
    return pl.pallas_call(
        attend_kernel,
        in_specs=[WHOLE] * 2,
        out_specs=WHOLE,
        out_shape=jax.ShapeDtypeStruct((ROWS, A), BF16),
        compiler_params=PARAMS,
        cost_estimate=pl.CostEstimate(
            flops=4 * HEADS * ROWS * 512 * HEAD, bytes_accessed=3 << 20, transcendentals=HEADS * ROWS * 512
        ),
    )(queries, kv)


def attend_back(lane, queries, grads, kv, token):
    return pl.pallas_call(
        attend_back_kernel,
        in_specs=[pl.BlockSpec(memory_space=pltpu.SMEM)] + [WHOLE] * 3 + [pl.BlockSpec(memory_space=pl.ANY)],
        out_specs=[WHOLE] * 5,
        out_shape=[jax.ShapeDtypeStruct((ROWS, A), BF16)]
        + [jax.ShapeDtypeStruct((ROWS, 2 * A), BF16)] * 4,
        scratch_shapes=[pltpu.VMEM((4, ROWS, 2 * A), BF16)],
        compiler_params=PARAMS,
        cost_estimate=pl.CostEstimate(
            flops=12 * HEADS * ROWS * 512 * HEAD, bytes_accessed=6 << 20, transcendentals=HEADS * ROWS * 512
        ),
    )(lane.reshape(1), queries, grads, kv, token)


def expert(rows, grad_act, gate, up):
    gate_pre = dot_nn(rows, gate)
    up_pre = dot_nn(rows, up)
    sigmoid_gate = jax.nn.sigmoid(gate_pre)
    silu_gate = gate_pre * sigmoid_gate
    activated = (silu_gate * up_pre).astype(BF16)
    grad_gate = (grad_act * up_pre * sigmoid_gate * (1.0 + gate_pre * (1.0 - sigmoid_gate))).astype(BF16)
    grad_up = (grad_act * silu_gate).astype(BF16)
    return activated, (dot_nt(grad_gate, gate) + dot_nt(grad_up, up)).astype(BF16)


def project_others_kernel(lane, right, opp, left, down, out):
    step = pl.program_id(0)

    @pl.when(step == 0)
    def _():
        out[...] = dot_nn(right[...], down[...]).astype(BF16)

    @pl.when(step == 1)
    def _():
        out[...] = dot_nn(opp[...], down[...]).astype(BF16)

    @pl.when(step == 2)
    def _():
        out[...] = dot_nn(left[...], down[...]).astype(BF16)


def project_others(lane, right, opp, left, down):
    return pl.pallas_call(
        project_others_kernel,
        grid_spec=pltpu.PrefetchScalarGridSpec(
            num_scalar_prefetch=1,
            grid=(3,),
            in_specs=[WHOLE] * 4,
            out_specs=pl.BlockSpec((POOL, D), lambda i, lane: ((lane[0] + 1 + i) % 4, 0)),
        ),
        out_shape=jax.ShapeDtypeStruct((4 * POOL, D), BF16),
        compiler_params=pltpu.CompilerParams(vmem_limit_bytes=48 << 20),
        cost_estimate=pl.CostEstimate(flops=6 * POOL * D * A, bytes_accessed=8 << 20, transcendentals=0),
    )(lane.reshape(1), right, opp, left, down)


def project_own_kernel(lane, own, down, others, token, out):
    out[...] = dot_nn(own[...], down[...]).astype(BF16)


def project_own(lane, own, down, others, token):
    anywhere = pl.BlockSpec(memory_space=pl.ANY)
    return pl.pallas_call(
        project_own_kernel,
        grid_spec=pltpu.PrefetchScalarGridSpec(
            num_scalar_prefetch=1,
            grid=(1,),
            in_specs=[WHOLE, WHOLE, anywhere, anywhere],
            out_specs=pl.BlockSpec((POOL, D), lambda i, lane: (lane[0], 0)),
        ),
        out_shape=jax.ShapeDtypeStruct((4 * POOL, D), BF16),
        input_output_aliases={3: 0},
        compiler_params=pltpu.CompilerParams(vmem_limit_bytes=48 << 20),
        cost_estimate=pl.CostEstimate(flops=2 * POOL * D * A, bytes_accessed=5 << 20, transcendentals=0),
    )(lane.reshape(1), own, down, others, token)


def row_of(me, turn, flip, core):
    return (((me // 4 - turn) % 4) * 4 + ((me // 2 % 2) ^ flip) * 2 + (me % 2 ^ core)) * 64


def shards(
    residual,
    queries,
    attn_keys,
    attn_values,
    out_weight,
    norm_gain,
    gate_weight,
    up_weight,
    down_weight,
    expert_ids,
    out_grad,
):
    gate, up, down = gate_weight[0], up_weight[0], down_weight[0]
    lane = lax.axis_index("dp")

    kv = lax.all_gather(jnp.concatenate([attn_keys, attn_values], axis=1), "dp", axis=0, tiled=True)

    expert_of = expert_ids[:, 0]
    onehot = (expert_of[:, None] == jnp.arange(EXPERTS, dtype=jnp.int32)[None, :]).astype(BF16)
    row = jnp.arange(ROWS, dtype=jnp.int32)
    earlier_mask = (row[:, None] > row[None, :]).astype(BF16)
    earlier = dot_nn(earlier_mask, onehot)
    rank = jnp.sum(earlier * onehot.astype(F32), axis=1).astype(jnp.int32)
    slot = expert_of * CAP + rank
    place = (jnp.arange(POOL, dtype=jnp.int32)[:, None] == slot[None, :]).astype(BF16)

    low_z = jnp.concatenate([out_weight[:32], *(along_z(out_weight[:32], k) for k in (1, 2, 3))], axis=0)
    high_y = jnp.concatenate([out_weight[32:], across_y(out_weight[32:])], axis=0)
    near_out = jnp.concatenate(
        [low_z, across_y(low_z), high_y, *(along_z(high_y, k) for k in (1, 2, 3))], axis=0
    )
    far_out = across_core(near_out)
    me = lax.axis_index("expert")
    row = jnp.arange(A, dtype=jnp.int32)
    part = row % 256
    in_high = (row // 256) % 2
    turn = jnp.where(in_high == 1, part // 64, (part // 32) % 4)
    flip = jnp.where(in_high == 1, (part // 32) % 2, part // 128)
    wanted = row_of(me, turn, flip, row // 512) + in_high * 32 + row % 32
    reorder = (row[:, None] == wanted[None, :]).astype(BF16)

    grad_buffer = dot_nn(place, out_grad).astype(BF16)
    grad_rows = lax.all_gather(swap_experts(grad_buffer), "dp", axis=0, tiled=True)

    attended = attend(queries, kv)
    ordered = dot_nn(attended, reorder).astype(BF16)
    hidden = residual.astype(F32) + dot_nn(ordered[:, : A // 2], near_out) + dot_nn(ordered[:, A // 2 :], far_out)
    inv_rms = lax.rsqrt(jnp.mean(hidden * hidden, axis=-1, keepdims=True) + EPSILON)
    unit_rows = hidden * inv_rms
    normed = (unit_rows * norm_gain).astype(BF16)

    rows_own = swap_experts(dot_nn(place, normed).astype(BF16))
    rows_left, rows_right = along_x(rows_own, 1), along_x(rows_own, 3)
    grad_act = dot_nt(grad_rows, down).reshape(4, POOL, A)

    def act_of(step):
        return lax.dynamic_index_in_dim(grad_act, (lane + step) % 4, 0, keepdims=False)

    act_own, part_own = expert(rows_own, act_of(0), gate, up)
    opp_low = along_x(after(rows_left[:HALF], act_own), 1)
    opp_high = along_x(after(rows_right[HALF:], act_own), 3)
    act_left, part_left = expert(rows_left, act_of(3), gate, up)
    act_right, part_right = expert(rows_right, act_of(1), gate, up)
    rows_opp = after(jnp.concatenate([opp_low, opp_high], axis=0), part_left, part_right)
    act_opp, part_opp = expert(rows_opp, act_of(2), gate, up)

    from_left = along_x(jnp.concatenate([part_opp[:HALF], part_right[HALF:]], axis=0), 1)
    from_right = along_x(jnp.concatenate([part_opp[HALF:], part_left[:HALF]], axis=0), 3)
    out_others = project_others(lane, act_right, act_opp, act_left, down)
    keep_right = (part_right[:HALF].astype(F32) + from_left[:HALF].astype(F32)).astype(BF16)
    keep_left = (part_left[HALF:].astype(F32) + from_right[:HALF].astype(F32)).astype(BF16)
    low_left = along_x(after(keep_right, out_others, part_own), 1)
    high_right = along_x(after(keep_left, out_others, part_own), 3)
    low_sum = low_left.astype(F32) + from_right[HALF:].astype(F32)
    high_sum = high_right.astype(F32) + from_left[HALF:].astype(F32)
    own_sum = (part_own.astype(F32) + jnp.concatenate([low_sum, high_sum], axis=0)).astype(BF16)
    grad_back = swap_experts(own_sum)

    out_part = project_own(lane, act_own, down, out_others, own_sum)
    out_sum = lax.psum_scatter(out_part, "dp", scatter_dimension=0, tiled=True)
    out_back = swap_experts(out_sum)

    scaled = dot_tn(place, grad_back) * norm_gain
    resid_grad = (
        out_grad.astype(F32)
        + inv_rms * (scaled - unit_rows * jnp.mean(scaled * unit_rows, axis=-1, keepdims=True))
    ).astype(BF16)

    grad_attended = jnp.concatenate([dot_nt(resid_grad, near_out), dot_nt(resid_grad, far_out)], axis=1)
    grad_attended = dot_nt(grad_attended.astype(BF16), reorder).astype(BF16)
    query_grad, kv_own, kv_right, kv_opp, kv_left = attend_back(lane, queries, grad_attended, kv, out_sum)
    kv_grad = (
        kv_own.astype(F32)
        + along_x(kv_opp, 2).astype(F32)
        + along_x(kv_right, 1).astype(F32)
        + along_x(kv_left, 3).astype(F32)
    ).astype(BF16)

    tile_attended = lax.all_gather(after(attended, part_left), "dp", axis=0, tiled=True)
    columns = lax.all_to_all(
        jnp.moveaxis(resid_grad.reshape(ROWS, 4, QUARTER), 1, 0), "dp", split_axis=0, concat_axis=0, tiled=True
    ).reshape(4 * ROWS, QUARTER)
    wanted = row_of(me, (row // 128) % 4, (row // 64) % 2, row // 512) + row % 64
    to_owner = (row[:, None] == wanted[None, :]).astype(BF16)
    tile_attended = dot_nn(tile_attended, to_owner).astype(BF16)
    partial = dot_tn(tile_attended[:, A // 2 :], columns).astype(BF16)
    kept = dot_tn(tile_attended[:, : A // 2], columns)
    partial = (kept + across_core(partial).astype(F32)).reshape(4, 128, QUARTER)
    low = partial.astype(BF16)
    partial = partial[0] + sum(along_z(low[k], 4 - k).astype(F32) for k in (1, 2, 3))
    low = partial.astype(BF16)
    pair = [(i, i ^ 16) for i in range(2 * EXPERTS)]
    cross = [(i, i ^ 18) for i in range(2 * EXPERTS)]
    low = (
        partial[:64]
        + across_y(low[64:]).astype(F32)
        + lax.ppermute(low[:64], ("section", "expert"), pair).astype(F32)
        + lax.ppermute(low[64:], ("section", "expert"), cross).astype(F32)
    ).astype(BF16)
    low = after(low, out_back)
    weight_grad = jnp.zeros((64, D), F32)
    for step in range(4):
        piece = low if step == 0 else along_x(low, step)
        weight_grad = lax.dynamic_update_slice(
            weight_grad, piece.astype(F32), (0, ((lane - step) % 4) * QUARTER)
        )

    layer_out = (hidden + dot_tn(place, out_back)).astype(BF16)
    return (layer_out, resid_grad, query_grad, kv_grad[:, :A], kv_grad[:, A:], weight_grad)


def solution(mesh):
    rows = P(("section", "expert", "dp"), None)
    return jax.shard_map(
        shards,
        mesh=mesh,
        in_specs=(
            rows,
            rows,
            rows,
            rows,
            P("expert", None),
            P(),
            P("expert", None, "dp"),
            P("expert", None, "dp"),
            P("expert", "dp", None),
            rows,
            rows,
        ),
        out_specs=(rows, rows, rows, rows, rows, P("expert", None)),
        check_vma=False,
    )
```
